32 devices in a mesh: cuts: 2 (over y), qa: 16 (over z, x, core).
Axes of the slice: x: 2, y: 2, z: 4, core: 2. Of those that a mesh axis runs over, the one named last changes fastest.
Arguments:
- state: float32 [2, 4194304], P(None, ('cuts', 'qa')), parts along dimension 1, may hold values from -6 to 6
- unitaries: float32 [12, 2, 128, 128], replicated, may hold values from -1 to 1, as said below
- gate_order: int32 [12], replicated, may hold values from 0 to 11, each once
- gate_starts: int32 [12], replicated, may hold values from 0 to 1
- pair_gates: float32 [2, 2, 2, 2], replicated, may hold values from -1 to 1, as said below
Outputs:
- final_state: float32 [2, 4194304], P(None, ('cuts', 'qa')), parts along dimension 1
The draws below stay inside these ranges and needn't reach their ends.
There are 2 independent parts, one for each index of `cuts`. The reference program is written for one: setup_inputs(seed, part) draws one part's arguments, and reference() takes and returns one part's arrays. A program takes and returns all parts, laid end to end along the dimension named above; an argument that names none is the same for every part. Nothing has to cross between parts.
Inputs may be any that keep to these rules, and one draw needn't show every extreme that they name: For every k, unitaries[k, 0] + i unitaries[k, 1] is a unitary matrix. For each p, pair_gates[p, 0] + i pair_gates[p, 1] is a unitary 2 x 2 matrix. `gate_order`: A permutation of 0 .. 11.
All inputs are finite; a program needn't handle non-finite values.
Results may differ from the reference program's by a relative error of at most 0.0003.
Values sent between devices are 32-bit elements; how exact they have to be, the bound alone decides.
A program may use at most 64 MiB of HBM per device.

```python
from functools import partial
import jax
import jax.numpy as jnp
from jax import lax

AMP_DEV = 131072
GDIM = 128
NGATES = 12
QA_DEVS = 16
AMPS = 2097152


def unitary_batch(key, count, dim):
    key_re, key_im = jax.random.split(jax.random.fold_in(key, 17))
    part_re = jax.random.normal(key_re, (count, dim, dim), jnp.float32)
    part_im = jax.random.normal(key_im, (count, dim, dim), jnp.float32)
    upper = jnp.concatenate([part_re, -part_im], axis=2)
    lower = jnp.concatenate([part_im, part_re], axis=2)
    embedded = jnp.concatenate([upper, lower], axis=1)
    left, values, right = jnp.linalg.svd(embedded)
    polar = jnp.matmul(left, right, precision=lax.Precision.HIGHEST)
    return jnp.stack([polar[:, :dim, :dim], polar[:, dim:, :dim]], axis=1)


def draw_unitaries(key, part):
    return unitary_batch(key, NGATES, GDIM).astype(jnp.float32)


def draw_pair_gates(key, part):
    return unitary_batch(jax.random.fold_in(key, 5), 2, 2).astype(jnp.float32)


def place_ends(drawn, rng, least, top_value):
    extent = drawn.shape
    index_at = [jax.random.randint(jax.random.fold_in(rng, axis), (), 0, extent[axis]) for axis in range(len(extent))]
    drawn = drawn.at[tuple(index_at)].set(least)
    longest = extent.index(max(extent))
    index_at[longest] = (index_at[longest] + 1) % extent[longest]
    return drawn.at[tuple(index_at)].set(top_value)


def steps_of(stream_key, dims, pieces, low, high):
    level = 1.0
    for dim, blocks in pieces:
        heights = jax.random.uniform(jax.random.fold_in(jax.random.fold_in(stream_key, 6), dim), (blocks,), jnp.float32, low / len(pieces), high / len(pieces))
        level = level * jnp.repeat(jnp.exp(heights), dims[dim] // blocks).reshape((-1,) + (1,) * (len(dims) - 1 - dim))
    return level


def gaussian(rng, dims, deviation, bound, cuts=(), kind=jnp.bfloat16):
    factor_of = steps_of(rng, dims, cuts, -0.22, 0.18) if cuts else 1.0
    values = jax.random.normal(rng, dims, jnp.float32) * deviation * factor_of
    return jnp.minimum(jnp.maximum(values, -bound), bound).astype(kind)


def setup_inputs(seed: int = 0, part: int = 0) -> dict:
    splits = jax.random.split(jax.random.key(seed), 6)
    part_splits = jax.random.split(jax.random.fold_in(splits[5], part), 6)
    return {
        "state": gaussian(part_splits[0], (2, AMPS), 1.0, 6.0, ((1, 16),), jnp.float32),
        "unitaries": draw_unitaries(jax.random.fold_in(splits[5], 71), part),
        "gate_order": jax.random.permutation(splits[2], NGATES).astype(jnp.int32),
        "gate_starts": place_ends(jax.random.randint(splits[3], (NGATES,), 0, 2), jax.random.fold_in(splits[3], 1), 0, 1).astype(jnp.int32),
        "pair_gates": draw_pair_gates(jax.random.fold_in(splits[5], 71), part),
    }


HIGH = lax.Precision.HIGHEST

def mix(mat, vec):
    return jnp.einsum('ij,ajb->aib', mat, vec, precision=HIGH)

def dense_branch(re_part, im_part, u_re, u_im, offset):
    gdim = u_re.shape[0]
    gq = gdim.bit_length() - 1
    block = 2 ** (gq + offset)
    shaped_re = re_part.reshape(-1, gdim, block)
    shaped_im = im_part.reshape(-1, gdim, block)
    new_re = mix(u_re, shaped_re) - mix(u_im, shaped_im)
    new_im = mix(u_re, shaped_im) + mix(u_im, shaped_re)
    return (new_re.reshape(-1), new_im.reshape(-1))

def dense_gate(stacked, unitaries, gate_order, gate_starts, k):
    chosen = unitaries[gate_order[k]]
    branches = [partial(dense_branch, offset=0), partial(dense_branch, offset=1)]
    new_re, new_im = lax.switch(gate_starts[k], branches, stacked[0], stacked[1], chosen[0], chosen[1])
    return jnp.stack([new_re, new_im])

def one_qubit(stacked, gate, qubit):
    shaped = stacked.reshape(2, -1, 2, 2 ** qubit)
    u_re, u_im = (gate[0], gate[1])
    new_re = jnp.einsum('bc,acx->abx', u_re, shaped[0], precision=HIGH) - jnp.einsum('bc,acx->abx', u_im, shaped[1], precision=HIGH)
    new_im = jnp.einsum('bc,acx->abx', u_re, shaped[1], precision=HIGH) + jnp.einsum('bc,acx->abx', u_im, shaped[0], precision=HIGH)
    return jnp.stack([new_re, new_im]).reshape(2, -1)

def qubit_swap(stacked):
    shaped = stacked.reshape(2, QA_DEVS, QA_DEVS, AMP_DEV // QA_DEVS)
    return jnp.transpose(shaped, (0, 2, 1, 3)).reshape(2, -1)

def reference(state, unitaries, gate_order, gate_starts, pair_gates):
    local_bits = AMP_DEV.bit_length() - 1
    global_bits = QA_DEVS.bit_length() - 1
    third = NGATES // 3
    stacked = state
    for k in range(third):
        stacked = dense_gate(stacked, unitaries, gate_order, gate_starts, k)
    stacked = qubit_swap(stacked)
    stacked = one_qubit(stacked, pair_gates[0], local_bits + global_bits - 1)
    for k in range(third, 2 * third):
        stacked = dense_gate(stacked, unitaries, gate_order, gate_starts, k)
    stacked = qubit_swap(stacked)
    stacked = one_qubit(stacked, pair_gates[1], local_bits)
    for k in range(2 * third, NGATES):
        stacked = dense_gate(stacked, unitaries, gate_order, gate_starts, k)
    return stacked
```

```python
import functools

import jax
import jax.numpy as jnp
from jax import lax
from jax.experimental import pallas as pl
from jax.experimental.pallas import tpu as pltpu
from jax.sharding import PartitionSpec as P

BF16 = jnp.bfloat16
F32 = jnp.float32


def split(x):
    hi = x.astype(BF16)
    return hi, (x - hi.astype(F32)).astype(BF16)


def dot(a, b):
    return jnp.dot(a, b, preferred_element_type=F32)


def embed(re, im):
    return jnp.concatenate(
        [jnp.concatenate([re, -im], axis=1), jnp.concatenate([im, re], axis=1)], axis=0
    )


def gate_matrix(u, order, k):
    re_hi, re_lo = split(u[order[k], 0])
    im_hi, im_lo = split(u[order[k], 1])
    return embed(re_hi, im_hi), embed(re_lo, im_lo)


def product(mat, x):
    hi, lo = mat
    x_hi, x_lo = split(x)
    return dot(hi, x_hi) + dot(hi, x_lo) + dot(lo, x_hi)


def relayout(y, plain, woven, old, new):
    gdim, lanes = y.shape[0] // 2, y.shape[1] // 2
    parts = [
        [y[r * gdim : (r + 1) * gdim, b * lanes : (b + 1) * lanes] for b in range(2)]
        for r in range(2)
    ]
    for r in range(2):
        for b in range(2):
            plain[r, b * gdim : (b + 1) * gdim, :] = parts[r][b]
            woven[r, pl.ds(b, gdim, stride=2), :] = parts[r][b]
    rows = []
    for r in range(2):
        cols = []
        for b in range(2):
            to_low = woven[r, b * gdim : (b + 1) * gdim, :]
            to_high = plain[r, pl.ds(b, gdim, stride=2), :]
            moved = jnp.where(old == 1, to_low, to_high)
            cols.append(jnp.where(old == new, parts[r][b], moved))
        rows.append(jnp.concatenate(cols, axis=1))
    return jnp.concatenate(rows, axis=0)


def run_gates(planes, mats, marks, plain, woven):
    gdim = planes[0].shape[0] // 2
    y = jnp.concatenate(
        [jnp.concatenate([p[:gdim], p[gdim:]], axis=1) for p in planes], axis=0
    )
    old = jnp.int32(0)
    for mat, new in zip(mats, marks):
        y = product(mat(), relayout(y, plain, woven, old, new))
        old = new
    y = relayout(y, plain, woven, old, jnp.int32(0))
    lanes = y.shape[1] // 2
    return [
        jnp.concatenate(
            [y[r * gdim : (r + 1) * gdim, :lanes], y[r * gdim : (r + 1) * gdim, lanes:]],
            axis=0,
        )
        for r in range(2)
    ]


def mix_pair(pair, p, b, low, high):
    r0, i0 = pair[p, 0, b, 0], pair[p, 1, b, 0]
    r1, i1 = pair[p, 0, b, 1], pair[p, 1, b, 1]
    re = r0 * low[0] - i0 * low[1] + (r1 * high[0] - i1 * high[1])
    im = r0 * low[1] + i0 * low[0] + (r1 * high[1] + i1 * high[0])
    return re, im


def compose(third, count, order, starts, u, plain, woven, w_hi, w_lo, after):
    rows, lanes = plain.shape[1], plain.shape[2]
    ks = [third * count + j for j in range(count)]
    built = [gate_matrix(u, order, k) for k in ks]
    for n in range(rows // lanes):
        at = lax.broadcasted_iota(jnp.int32, (rows, lanes), 0)
        col = lax.broadcasted_iota(jnp.int32, (rows, lanes), 1) + n * lanes
        one = jnp.where(at == col, 1.0, 0.0).astype(F32)
        planes = run_gates(
            [one, jnp.zeros_like(one)],
            [lambda m=m: m for m in built],
            [starts[k] for k in ks],
            plain,
            woven,
        )
        re, im = after(planes)
        for out, r, i in zip((w_hi, w_lo), split(re), split(im)):
            here = slice(n * lanes, (n + 1) * lanes)
            there = slice(rows + n * lanes, rows + (n + 1) * lanes)
            out[:rows, here] = r
            out[rows:, there] = r
            out[rows:, here] = i
            out[:rows, there] = -i


def apply(w_hi, w_lo, x):
    lanes = x.shape[1]
    x_hi, x_lo = split(x)
    both = dot(w_hi[...], jnp.concatenate([x_hi, x_lo], axis=1))
    return both[:, :lanes] + both[:, lanes:] + dot(w_lo[...], x_hi)


def kernel(
    group, pair_bit, order, starts, pair, x_hbm, u_hbm, o_hbm,
    x_in, u, first_hi, first_lo, plain, woven, w_hi, w_lo,
    sent, got, x_out, in_sem, out_sem, send_sem, recv_sem,
):
    chunks, rows, lanes = x_in.shape[0], x_in.shape[1] // 2, x_in.shape[2]
    count = u.shape[0] // 3
    block = rows // group
    index = lax.axis_index("qa")
    me = lax.rem(index, group)
    base = index - me

    barrier = pltpu.get_barrier_semaphore()
    for d in range(1, group):
        pl.semaphore_signal(
            barrier, inc=1, device_id={"qa": base + lax.rem(me + d, group)},
            device_id_type=pl.DeviceIdType.MESH,
        )
    load_u = pltpu.make_async_copy(u_hbm, u, in_sem.at[0])
    load_x = pltpu.make_async_copy(x_hbm, x_in, in_sem.at[1])
    load_u.start()
    load_x.start()
    load_u.wait()
    for k in range(count):
        first_hi[k], first_lo[k] = gate_matrix(u, order, k)
    load_x.wait()

    def block_at(j):
        return pl.ds(pl.multiple_of(j * block, block), block)

    def remote(phase, c, d):
        peer = lax.rem(me + d, group)
        return pltpu.make_async_remote_copy(
            src_ref=sent.at[phase, c, :, block_at(peer), :],
            dst_ref=got.at[phase, c, :, block_at(me), :],
            send_sem=send_sem.at[phase, c, d],
            recv_sem=recv_sem.at[phase, c, d],
            device_id={"qa": base + peer},
            device_id_type=pl.DeviceIdType.MESH,
        )

    def exchange(phase, c):
        def one(d, _):
            remote(phase, c, d).start()
            return 0

        lax.fori_loop(1, group, one, 0)
        got[phase, c, :, block_at(me), :] = sent[phase, c, :, block_at(me), :]

    def arrived(phase, c):
        def one(d, _):
            remote(phase, c, d).wait_recv()
            return 0

        lax.fori_loop(1, group, one, 0)

    def first_gates(c):
        half = chunks // 2
        low, high = lax.rem(c, half), lax.rem(c, half) + half

        def planes_of(n):
            return [x_in[n, pl.ds(r, rows, stride=2), :] for r in range(2)]

        planes = mix_pair(pair, 0, c // half, planes_of(low), planes_of(high))
        done = run_gates(
            planes,
            [lambda k=k: (first_hi[k], first_lo[k]) for k in range(count)],
            [starts[k] for k in range(count)],
            plain,
            woven,
        )
        for r in range(2):
            sent[0, c, r] = done[r]

    first_gates(jnp.int32(0))
    pl.semaphore_wait(barrier, group - 1)
    exchange(0, jnp.int32(0))

    def first(c, _):
        first_gates(c)
        exchange(0, c)
        return 0

    lax.fori_loop(1, chunks, first, 0)

    def with_pair(planes):
        pieces = ([], [])
        for start in range(0, rows, 2 * pair_bit):
            low = [p[start : start + pair_bit] for p in planes]
            high = [p[start + pair_bit : start + 2 * pair_bit] for p in planes]
            for b in range(2):
                for out, part in zip(pieces, mix_pair(pair, 1, b, low, high)):
                    out.append(part)
        return [jnp.concatenate(p, axis=0) for p in pieces]

    compose(1, count, order, starts, u, plain, woven, w_hi, w_lo, with_pair)

    def second(c, _):
        arrived(0, c)
        y = apply(w_hi, w_lo, got[0, c].reshape(2 * rows, lanes))
        sent[1, c] = y.reshape(2, rows, lanes)
        exchange(1, c)
        return 0

    lax.fori_loop(0, chunks, second, 0)

    compose(2, count, order, starts, u, plain, woven, w_hi, w_lo, lambda p: p)

    def store(c):
        return pltpu.make_async_copy(x_out.at[c], o_hbm.at[c], out_sem.at[c])

    def last(c, _):
        arrived(1, c)
        y = apply(w_hi, w_lo, got[1, c].reshape(2 * rows, lanes))
        for r in range(2):
            x_out[c, pl.ds(r, rows, stride=2), :] = y[r * rows : (r + 1) * rows]
        store(c).start()
        return 0

    lax.fori_loop(0, chunks, last, 0)

    def finish(c, _):
        store(c).wait()
        for phase in range(2):
            lax.fori_loop(
                1, group, lambda d, _: (remote(phase, c, d).wait_send(), 0)[1], 0
            )
        return 0

    lax.fori_loop(0, chunks, finish, 0)


def shards(state, unitaries, gate_order, gate_starts, pair_gates):
    amp_local = state.shape[1]
    gdim = unitaries.shape[-1]
    ngates = unitaries.shape[0]
    rows, lanes = 2 * gdim, gdim
    chunks = amp_local // (rows * lanes)
    unit = amp_local // lax.axis_size("qa")
    group = rows * lanes // unit
    x = state.reshape(2, chunks * rows, lanes).transpose(1, 0, 2)
    x = x.reshape(chunks, 2 * rows, lanes)
    smem = pl.BlockSpec(memory_space=pltpu.SMEM)
    hbm = pl.BlockSpec(memory_space=pl.ANY)
    y = pl.pallas_call(
        functools.partial(kernel, group, unit // lanes),
        out_shape=jax.ShapeDtypeStruct(x.shape, F32),
        in_specs=[smem, smem, smem, hbm, hbm],
        out_specs=hbm,
        scratch_shapes=[
            pltpu.VMEM(x.shape, F32),
            pltpu.VMEM(unitaries.shape, F32),
            pltpu.VMEM((ngates // 3, 2 * gdim, 2 * gdim), BF16),
            pltpu.VMEM((ngates // 3, 2 * gdim, 2 * gdim), BF16),
            pltpu.VMEM((2, rows, lanes), F32),
            pltpu.VMEM((2, rows, lanes), F32),
            pltpu.VMEM((2 * rows, 2 * rows), BF16),
            pltpu.VMEM((2 * rows, 2 * rows), BF16),
            pltpu.VMEM((2, chunks, 2, rows, lanes), F32),
            pltpu.VMEM((2, chunks, 2, rows, lanes), F32),
            pltpu.VMEM(x.shape, F32),
            pltpu.SemaphoreType.DMA((2,)),
            pltpu.SemaphoreType.DMA((chunks,)),
            pltpu.SemaphoreType.DMA((2, chunks, group)),
            pltpu.SemaphoreType.DMA((2, chunks, group)),
        ],
        compiler_params=pltpu.CompilerParams(
            collective_id=0, has_side_effects=True, vmem_limit_bytes=40 * 2**20
        ),
        cost_estimate=pl.CostEstimate(
            flops=8 * 14 * chunks * rows * lanes * gdim,
            bytes_accessed=8 * amp_local * 2, transcendentals=0,
        ),
    )(gate_order, gate_starts, pair_gates, x, unitaries)
    y = y.reshape(chunks * rows, 2, lanes).transpose(1, 0, 2)
    return y.reshape(2, amp_local)


def solution(mesh):
    placed = (P(None, ("cuts", "qa")), P(), P(), P(), P())
    return jax.shard_map(
        shards, mesh=mesh, in_specs=placed, out_specs=P(None, ("cuts", "qa")), check_vma=False
    )
```

```python
import functools

import jax
import jax.numpy as jnp
from jax import lax
from jax.experimental import pallas as pl
from jax.experimental.pallas import tpu as pltpu
from jax.sharding import PartitionSpec as P

VMEM = 63 * 2**20
BF16 = jnp.bfloat16
F32 = jnp.float32


def split(x):
    hi = x.astype(BF16)
    return hi, (x - hi.astype(F32)).astype(BF16)


def dot(a, b):
    return jnp.dot(a, b, preferred_element_type=F32)


def embed(re, im):
    return jnp.concatenate(
        [jnp.concatenate([re, -im], axis=1), jnp.concatenate([im, re], axis=1)], axis=0
    )


def gate_matrix(u, order, k):
    re_hi, re_lo = split(u[order[k], 0])
    im_hi, im_lo = split(u[order[k], 1])
    return embed(re_hi, im_hi), embed(re_lo, im_lo)


def product(mat, x):
    hi, lo = mat
    x_hi, x_lo = split(x)
    return dot(hi, x_hi) + dot(hi, x_lo) + dot(lo, x_hi)


def relayout(y, plain, woven, old, new):
    gdim, lanes = y.shape[0] // 2, y.shape[1] // 2
    parts = [
        [y[r * gdim : (r + 1) * gdim, b * lanes : (b + 1) * lanes] for b in range(2)]
        for r in range(2)
    ]
    for r in range(2):
        for b in range(2):
            plain[r, b * gdim : (b + 1) * gdim, :] = parts[r][b]
            woven[r, pl.ds(b, gdim, stride=2), :] = parts[r][b]
    rows = []
    for r in range(2):
        cols = []
        for b in range(2):
            to_low = woven[r, b * gdim : (b + 1) * gdim, :]
            to_high = plain[r, pl.ds(b, gdim, stride=2), :]
            moved = jnp.where(old == 1, to_low, to_high)
            cols.append(jnp.where(old == new, parts[r][b], moved))
        rows.append(jnp.concatenate(cols, axis=1))
    return jnp.concatenate(rows, axis=0)


def run_gates(planes, mats, marks, plain, woven):
    gdim = planes[0].shape[0] // 2
    y = jnp.concatenate(
        [jnp.concatenate([p[:gdim], p[gdim:]], axis=1) for p in planes], axis=0
    )
    old = jnp.int32(0)
    for mat, new in zip(mats, marks):
        y = product(mat(), relayout(y, plain, woven, old, new))
        old = new
    y = relayout(y, plain, woven, old, jnp.int32(0))
    lanes = y.shape[1] // 2
    return [
        jnp.concatenate(
            [y[r * gdim : (r + 1) * gdim, :lanes], y[r * gdim : (r + 1) * gdim, lanes:]],
            axis=0,
        )
        for r in range(2)
    ]


def mix_pair(pair, p, b, low, high):
    r0, i0 = pair[p, 0, b, 0], pair[p, 1, b, 0]
    r1, i1 = pair[p, 0, b, 1], pair[p, 1, b, 1]
    re = r0 * low[0] - i0 * low[1] + (r1 * high[0] - i1 * high[1])
    im = r0 * low[1] + i0 * low[0] + (r1 * high[1] + i1 * high[0])
    return re, im


def compose(third, count, order, starts, u, plain, woven, w_hi, w_lo, after):
    rows, lanes = plain.shape[1], plain.shape[2]
    ks = [third * count + j for j in range(count)]
    built = [gate_matrix(u, order, k) for k in ks]
    for n in range(rows // lanes):
        at = lax.broadcasted_iota(jnp.int32, (rows, lanes), 0)
        col = lax.broadcasted_iota(jnp.int32, (rows, lanes), 1) + n * lanes
        one = jnp.where(at == col, 1.0, 0.0).astype(F32)
        planes = run_gates(
            [one, jnp.zeros_like(one)],
            [lambda m=m: m for m in built],
            [starts[k] for k in ks],
            plain,
            woven,
        )
        re, im = after(planes)
        for out, r, i in zip((w_hi, w_lo), split(re), split(im)):
            here = slice(n * lanes, (n + 1) * lanes)
            there = slice(rows + n * lanes, rows + (n + 1) * lanes)
            out[:rows, here] = r
            out[rows:, there] = r
            out[rows:, here] = i
            out[:rows, there] = -i


def apply(w_hi, w_lo, x):
    lanes = x.shape[1]
    x_hi, x_lo = split(x)
    both = dot(w_hi[...], jnp.concatenate([x_hi, x_lo], axis=1))
    return both[:, :lanes] + both[:, lanes:] + dot(w_lo[...], x_hi)


def kernel(
    group, pair_bit, order_hbm, starts_hbm, pair_hbm, x_hbm, u_hbm, o_hbm,
    order, starts, pair, x_in, u, first_hi, first_lo, plain, woven, w_hi, w_lo,
    sent, got, x_out, in_sem, out_sem, send_sem, recv_sem,
):
    chunks, rows, lanes = x_in.shape[0], x_in.shape[1] // 2, x_in.shape[2]
    count = u.shape[0] // 3
    block = rows // group
    index = lax.axis_index("qa")
    me = lax.rem(index, group)
    base = index - me

    small = [
        pltpu.make_async_copy(src, dst, in_sem.at[n])
        for n, (src, dst) in enumerate(
            [(order_hbm, order), (starts_hbm, starts), (pair_hbm, pair)]
        )
    ]
    load_u = pltpu.make_async_copy(u_hbm, u, in_sem.at[3])
    load_x = pltpu.make_async_copy(x_hbm, x_in, in_sem.at[4])
    for load in small + [load_u, load_x]:
        load.start()
    barrier = pltpu.get_barrier_semaphore()
    for d in range(1, group):
        pl.semaphore_signal(
            barrier, inc=1, device_id={"qa": base + lax.rem(me + d, group)},
            device_id_type=pl.DeviceIdType.MESH,
        )
    for load in small + [load_u]:
        load.wait()
    for k in range(count):
        first_hi[k], first_lo[k] = gate_matrix(u, order, k)
    load_x.wait()

    def block_at(j):
        return pl.ds(pl.multiple_of(j * block, block), block)

    def remote(phase, c, d):
        peer = lax.rem(me + d, group)
        return pltpu.make_async_remote_copy(
            src_ref=sent.at[phase, c, :, block_at(peer), :],
            dst_ref=got.at[phase, c, :, block_at(me), :],
            send_sem=send_sem.at[phase, c, d],
            recv_sem=recv_sem.at[phase, c, d],
            device_id={"qa": base + peer},
            device_id_type=pl.DeviceIdType.MESH,
        )

    def exchange(phase, c):
        def one(d, _):
            remote(phase, c, d).start()
            return 0

        lax.fori_loop(1, group, one, 0)
        got[phase, c, :, block_at(me), :] = sent[phase, c, :, block_at(me), :]

    def arrived(phase, c):
        def one(d, _):
            remote(phase, c, d).wait_recv()
            return 0

        lax.fori_loop(1, group, one, 0)

    def first_gates(c):
        half = chunks // 2
        low, high = lax.rem(c, half), lax.rem(c, half) + half

        def planes_of(n):
            return [x_in[n, pl.ds(r, rows, stride=2), :] for r in range(2)]

        planes = mix_pair(pair, 0, c // half, planes_of(low), planes_of(high))
        done = run_gates(
            planes,
            [lambda k=k: (first_hi[k], first_lo[k]) for k in range(count)],
            [starts[k] for k in range(count)],
            plain,
            woven,
        )
        for r in range(2):
            sent[0, c, r] = done[r]

    first_gates(jnp.int32(0))
    pl.semaphore_wait(barrier, group - 1)
    exchange(0, jnp.int32(0))

    def first(c, _):
        first_gates(c)
        exchange(0, c)
        return 0

    lax.fori_loop(1, chunks, first, 0)

    def with_pair(planes):
        pieces = ([], [])
        for start in range(0, rows, 2 * pair_bit):
            low = [p[start : start + pair_bit] for p in planes]
            high = [p[start + pair_bit : start + 2 * pair_bit] for p in planes]
            for b in range(2):
                for out, part in zip(pieces, mix_pair(pair, 1, b, low, high)):
                    out.append(part)
        return [jnp.concatenate(p, axis=0) for p in pieces]

    compose(1, count, order, starts, u, plain, woven, w_hi, w_lo, with_pair)

    def second(c, _):
        arrived(0, c)
        y = apply(w_hi, w_lo, got[0, c].reshape(2 * rows, lanes))
        sent[1, c] = y.reshape(2, rows, lanes)
        exchange(1, c)
        return 0

    lax.fori_loop(0, chunks, second, 0)

    compose(2, count, order, starts, u, plain, woven, w_hi, w_lo, lambda p: p)

    def store(c):
        return pltpu.make_async_copy(x_out.at[c], o_hbm.at[c], out_sem.at[c])

    def last(c, _):
        arrived(1, c)
        y = apply(w_hi, w_lo, got[1, c].reshape(2 * rows, lanes))
        for r in range(2):
            x_out[c, pl.ds(r, rows, stride=2), :] = y[r * rows : (r + 1) * rows]
        store(c).start()
        return 0

    lax.fori_loop(0, chunks, last, 0)

    def finish(c, _):
        store(c).wait()
        for phase in range(2):
            lax.fori_loop(
                1, group, lambda d, _: (remote(phase, c, d).wait_send(), 0)[1], 0
            )
        return 0

    lax.fori_loop(0, chunks, finish, 0)


def shards(state, unitaries, gate_order, gate_starts, pair_gates):
    amp_local = state.shape[1]
    gdim = unitaries.shape[-1]
    ngates = unitaries.shape[0]
    rows, lanes = 2 * gdim, gdim
    chunks = amp_local // (rows * lanes)
    unit = amp_local // lax.axis_size("qa")
    group = rows * lanes // unit
    x = state.reshape(2, chunks * rows, lanes).transpose(1, 0, 2)
    x = x.reshape(chunks, 2 * rows, lanes)
    hbm = pl.BlockSpec(memory_space=pltpu.HBM)
    y = pl.pallas_call(
        functools.partial(kernel, group, unit // lanes),
        out_shape=jax.ShapeDtypeStruct(x.shape, F32),
        in_specs=[hbm] * 5,
        out_specs=pl.BlockSpec(memory_space=pl.ANY),
        scratch_shapes=[
            pltpu.SMEM(gate_order.shape, jnp.int32),
            pltpu.SMEM(gate_starts.shape, jnp.int32),
            pltpu.SMEM(pair_gates.shape, F32),
            pltpu.VMEM(x.shape, F32),
            pltpu.VMEM(unitaries.shape, F32),
            pltpu.VMEM((ngates // 3, 2 * gdim, 2 * gdim), BF16),
            pltpu.VMEM((ngates // 3, 2 * gdim, 2 * gdim), BF16),
            pltpu.VMEM((2, rows, lanes), F32),
            pltpu.VMEM((2, rows, lanes), F32),
            pltpu.VMEM((2 * rows, 2 * rows), BF16),
            pltpu.VMEM((2 * rows, 2 * rows), BF16),
            pltpu.VMEM((2, chunks, 2, rows, lanes), F32),
            pltpu.VMEM((2, chunks, 2, rows, lanes), F32),
            pltpu.VMEM(x.shape, F32),
            pltpu.SemaphoreType.DMA((5,)),
            pltpu.SemaphoreType.DMA((chunks,)),
            pltpu.SemaphoreType.DMA((2, chunks, group)),
            pltpu.SemaphoreType.DMA((2, chunks, group)),
        ],
        compiler_params=pltpu.CompilerParams(
            collective_id=0, has_side_effects=True, vmem_limit_bytes=VMEM
        ),
        cost_estimate=pl.CostEstimate(
            flops=8 * 14 * chunks * rows * lanes * gdim,
            bytes_accessed=8 * amp_local * 2, transcendentals=0,
        ),
    )(gate_order, gate_starts, pair_gates, x, unitaries)
    y = y.reshape(chunks * rows, 2, lanes).transpose(1, 0, 2)
    return y.reshape(2, amp_local)


def solution(mesh):
    placed = (P(None, ("cuts", "qa")), P(), P(), P(), P())
    return jax.shard_map(
        shards, mesh=mesh, in_specs=placed, out_specs=P(None, ("cuts", "qa")), check_vma=False
    )
```

```python
import functools

import jax
import jax.numpy as jnp
from jax import lax
from jax.experimental import pallas as pl
from jax.experimental.pallas import tpu as pltpu
from jax.sharding import PartitionSpec as P

VMEM = 40 * 2**20
BF16 = jnp.bfloat16
F32 = jnp.float32


def split(x):
    hi = x.astype(BF16)
    return hi, (x - hi.astype(F32)).astype(BF16)


def dot(a, b):
    return jnp.dot(a, b, preferred_element_type=F32)


def embed(re, im):
    return jnp.concatenate(
        [jnp.concatenate([re, -im], axis=1), jnp.concatenate([im, re], axis=1)], axis=0
    )


def gate_matrix(u, order, k):
    re_hi, re_lo = split(u[order[k], 0])
    im_hi, im_lo = split(u[order[k], 1])
    return embed(re_hi, im_hi), embed(re_lo, im_lo)


def product(mat, x):
    hi, lo = mat
    x_hi, x_lo = split(x)
    return dot(hi, x_hi) + dot(hi, x_lo) + dot(lo, x_hi)


def relayout(y, plain, woven, old, new):
    gdim, lanes = y.shape[0] // 2, y.shape[1] // 2
    parts = [
        [y[r * gdim : (r + 1) * gdim, b * lanes : (b + 1) * lanes] for b in range(2)]
        for r in range(2)
    ]
    for r in range(2):
        for b in range(2):
            plain[r, b * gdim : (b + 1) * gdim, :] = parts[r][b]
            woven[r, pl.ds(b, gdim, stride=2), :] = parts[r][b]
    rows = []
    for r in range(2):
        cols = []
        for b in range(2):
            to_low = woven[r, b * gdim : (b + 1) * gdim, :]
            to_high = plain[r, pl.ds(b, gdim, stride=2), :]
            moved = jnp.where(old == 1, to_low, to_high)
            cols.append(jnp.where(old == new, parts[r][b], moved))
        rows.append(jnp.concatenate(cols, axis=1))
    return jnp.concatenate(rows, axis=0)


def run_gates(planes, mats, marks, plain, woven):
    gdim = planes[0].shape[0] // 2
    y = jnp.concatenate(
        [jnp.concatenate([p[:gdim], p[gdim:]], axis=1) for p in planes], axis=0
    )
    old = jnp.int32(0)
    for mat, new in zip(mats, marks):
        y = product(mat(), relayout(y, plain, woven, old, new))
        old = new
    y = relayout(y, plain, woven, old, jnp.int32(0))
    lanes = y.shape[1] // 2
    return [
        jnp.concatenate(
            [y[r * gdim : (r + 1) * gdim, :lanes], y[r * gdim : (r + 1) * gdim, lanes:]],
            axis=0,
        )
        for r in range(2)
    ]


def mix_pair(pair, p, b, low, high):
    r0, i0 = pair[p, 0, b, 0], pair[p, 1, b, 0]
    r1, i1 = pair[p, 0, b, 1], pair[p, 1, b, 1]
    re = r0 * low[0] - i0 * low[1] + (r1 * high[0] - i1 * high[1])
    im = r0 * low[1] + i0 * low[0] + (r1 * high[1] + i1 * high[0])
    return re, im


def compose(third, count, order, starts, u, plain, woven, w_hi, w_lo, after):
    rows, lanes = plain.shape[1], plain.shape[2]
    ks = [third * count + j for j in range(count)]
    built = [gate_matrix(u, order, k) for k in ks]
    for n in range(rows // lanes):
        at = lax.broadcasted_iota(jnp.int32, (rows, lanes), 0)
        col = lax.broadcasted_iota(jnp.int32, (rows, lanes), 1) + n * lanes
        one = jnp.where(at == col, 1.0, 0.0).astype(F32)
        planes = run_gates(
            [one, jnp.zeros_like(one)],
            [lambda m=m: m for m in built],
            [starts[k] for k in ks],
            plain,
            woven,
        )
        re, im = after(planes)
        for out, r, i in zip((w_hi, w_lo), split(re), split(im)):
            here = slice(n * lanes, (n + 1) * lanes)
            there = slice(rows + n * lanes, rows + (n + 1) * lanes)
            out[:rows, here] = r
            out[rows:, there] = r
            out[rows:, here] = i
            out[:rows, there] = -i


def apply(w_hi, w_lo, x):
    lanes = x.shape[1]
    x_hi, x_lo = split(x)
    both = dot(w_hi[...], jnp.concatenate([x_hi, x_lo], axis=1))
    return both[:, :lanes] + both[:, lanes:] + dot(w_lo[...], x_hi)


def kernel(
    group, pair_bit, order_hbm, starts_hbm, pair_hbm, x_hbm, u_hbm, x_out,
    order, starts, pair, x_in, u, first_hi, first_lo, plain, woven, w_hi, w_lo,
    sent, got, in_sem, send_sem, recv_sem,
):
    chunks, rows, lanes = x_in.shape[0], x_in.shape[1] // 2, x_in.shape[2]
    count = u.shape[0] // 3
    block = rows // group
    index = lax.axis_index("qa")
    me = lax.rem(index, group)
    base = index - me

    small = [
        pltpu.make_async_copy(src, dst, in_sem.at[n])
        for n, (src, dst) in enumerate(
            [(order_hbm, order), (starts_hbm, starts), (pair_hbm, pair)]
        )
    ]
    load_u = pltpu.make_async_copy(u_hbm, u, in_sem.at[3])
    load_x = pltpu.make_async_copy(x_hbm, x_in, in_sem.at[4])
    for load in small + [load_u, load_x]:
        load.start()
    barrier = pltpu.get_barrier_semaphore()
    for d in range(1, group):
        pl.semaphore_signal(
            barrier, inc=1, device_id={"qa": base + lax.rem(me + d, group)},
            device_id_type=pl.DeviceIdType.MESH,
        )
    for load in small + [load_u]:
        load.wait()
    for k in range(count):
        first_hi[k], first_lo[k] = gate_matrix(u, order, k)
    load_x.wait()

    def block_at(j):
        return pl.ds(pl.multiple_of(j * block, block), block)

    def remote(phase, c, d):
        peer = lax.rem(me + d, group)
        return pltpu.make_async_remote_copy(
            src_ref=sent.at[phase, c, :, block_at(peer), :],
            dst_ref=got.at[phase, c, :, block_at(me), :],
            send_sem=send_sem.at[phase, c, d],
            recv_sem=recv_sem.at[phase, c, d],
            device_id={"qa": base + peer},
            device_id_type=pl.DeviceIdType.MESH,
        )

    def exchange(phase, c):
        def one(d, _):
            remote(phase, c, d).start()
            return 0

        lax.fori_loop(1, group, one, 0)
        got[phase, c, :, block_at(me), :] = sent[phase, c, :, block_at(me), :]

    def arrived(phase, c):
        def one(d, _):
            remote(phase, c, d).wait_recv()
            return 0

        lax.fori_loop(1, group, one, 0)

    def first_gates(c):
        half = chunks // 2
        low, high = lax.rem(c, half), lax.rem(c, half) + half

        def planes_of(n):
            return [x_in[n, pl.ds(r, rows, stride=2), :] for r in range(2)]

        planes = mix_pair(pair, 0, c // half, planes_of(low), planes_of(high))
        done = run_gates(
            planes,
            [lambda k=k: (first_hi[k], first_lo[k]) for k in range(count)],
            [starts[k] for k in range(count)],
            plain,
            woven,
        )
        for r in range(2):
            sent[0, c, r] = done[r]

    first_gates(jnp.int32(0))
    pl.semaphore_wait(barrier, group - 1)
    exchange(0, jnp.int32(0))

    def first(c, _):
        first_gates(c)
        exchange(0, c)
        return 0

    lax.fori_loop(1, chunks, first, 0)

    def with_pair(planes):
        pieces = ([], [])
        for start in range(0, rows, 2 * pair_bit):
            low = [p[start : start + pair_bit] for p in planes]
            high = [p[start + pair_bit : start + 2 * pair_bit] for p in planes]
            for b in range(2):
                for out, part in zip(pieces, mix_pair(pair, 1, b, low, high)):
                    out.append(part)
        return [jnp.concatenate(p, axis=0) for p in pieces]

    compose(1, count, order, starts, u, plain, woven, w_hi, w_lo, with_pair)

    def second(c, _):
        arrived(0, c)
        y = apply(w_hi, w_lo, got[0, c].reshape(2 * rows, lanes))
        sent[1, c] = y.reshape(2, rows, lanes)
        exchange(1, c)
        return 0

    lax.fori_loop(0, chunks, second, 0)

    compose(2, count, order, starts, u, plain, woven, w_hi, w_lo, lambda p: p)

    def last(c, _):
        arrived(1, c)
        y = apply(w_hi, w_lo, got[1, c].reshape(2 * rows, lanes))
        for r in range(2):
            x_out[c, pl.ds(r, rows, stride=2), :] = y[r * rows : (r + 1) * rows]
        return 0

    lax.fori_loop(0, chunks, last, 0)

    def finish(c, _):
        for phase in range(2):
            lax.fori_loop(
                1, group, lambda d, _: (remote(phase, c, d).wait_send(), 0)[1], 0
            )
        return 0

    lax.fori_loop(0, chunks, finish, 0)


def shards(state, unitaries, gate_order, gate_starts, pair_gates):
    amp_local = state.shape[1]
    gdim = unitaries.shape[-1]
    ngates = unitaries.shape[0]
    rows, lanes = 2 * gdim, gdim
    chunks = amp_local // (rows * lanes)
    unit = amp_local // lax.axis_size("qa")
    group = rows * lanes // unit
    x = state.reshape(2, chunks * rows, lanes).transpose(1, 0, 2)
    x = x.reshape(chunks, 2 * rows, lanes)
    hbm = pl.BlockSpec(memory_space=pltpu.HBM)
    y = pl.pallas_call(
        functools.partial(kernel, group, unit // lanes),
        out_shape=pltpu.VMEM(x.shape, F32),
        in_specs=[hbm] * 5,
        out_specs=pl.BlockSpec(memory_space=pltpu.VMEM),
        scratch_shapes=[
            pltpu.SMEM(gate_order.shape, jnp.int32),
            pltpu.SMEM(gate_starts.shape, jnp.int32),
            pltpu.SMEM(pair_gates.shape, F32),
            pltpu.VMEM(x.shape, F32),
            pltpu.VMEM(unitaries.shape, F32),
            pltpu.VMEM((ngates // 3, 2 * gdim, 2 * gdim), BF16),
            pltpu.VMEM((ngates // 3, 2 * gdim, 2 * gdim), BF16),
            pltpu.VMEM((2, rows, lanes), F32),
            pltpu.VMEM((2, rows, lanes), F32),
            pltpu.VMEM((2 * rows, 2 * rows), BF16),
            pltpu.VMEM((2 * rows, 2 * rows), BF16),
            pltpu.VMEM((2, chunks, 2, rows, lanes), F32),
            pltpu.VMEM((2, chunks, 2, rows, lanes), F32),
            pltpu.SemaphoreType.DMA((5,)),
            pltpu.SemaphoreType.DMA((2, chunks, group)),
            pltpu.SemaphoreType.DMA((2, chunks, group)),
        ],
        compiler_params=pltpu.CompilerParams(
            collective_id=0, has_side_effects=True, vmem_limit_bytes=VMEM
        ),
        cost_estimate=pl.CostEstimate(
            flops=8 * 14 * chunks * rows * lanes * gdim,
            bytes_accessed=8 * amp_local * 2, transcendentals=0,
        ),
    )(*(
        pltpu.with_memory_space_constraint(a, pltpu.HBM)
        for a in (gate_order, gate_starts, pair_gates, x, unitaries)
    ))
    y = y.reshape(chunks * rows, 2, lanes).transpose(1, 0, 2)
    return y.reshape(2, amp_local)


def solution(mesh):
    placed = (P(None, ("cuts", "qa")), P(), P(), P(), P())
    return jax.shard_map(
        shards, mesh=mesh, in_specs=placed, out_specs=P(None, ("cuts", "qa")), check_vma=False
    )
```

```python
import functools

import jax
import jax.numpy as jnp
from jax import lax
from jax.experimental import pallas as pl
from jax.experimental.pallas import tpu as pltpu
from jax.sharding import PartitionSpec as P

VMEM = 40 * 2**20
BF16 = jnp.bfloat16
F32 = jnp.float32


def split(x):
    hi = x.astype(BF16)
    return hi, (x - hi.astype(F32)).astype(BF16)


def dot(a, b):
    return jnp.dot(a, b, preferred_element_type=F32)


def embed(re, im):
    return jnp.concatenate(
        [jnp.concatenate([re, -im], axis=1), jnp.concatenate([im, re], axis=1)], axis=0
    )


def gate_matrix(u, order, k):
    re_hi, re_lo = split(u[order[k], 0])
    im_hi, im_lo = split(u[order[k], 1])
    return embed(re_hi, im_hi), embed(re_lo, im_lo)


def product(mat, x):
    hi, lo = mat
    x_hi, x_lo = split(x)
    return dot(hi, x_hi) + dot(hi, x_lo) + dot(lo, x_hi)


def relayout(y, plain, woven, old, new):
    gdim, lanes = y.shape[0] // 2, y.shape[1] // 2
    parts = [
        [y[r * gdim : (r + 1) * gdim, b * lanes : (b + 1) * lanes] for b in range(2)]
        for r in range(2)
    ]
    for r in range(2):
        for b in range(2):
            plain[r, b * gdim : (b + 1) * gdim, :] = parts[r][b]
            woven[r, pl.ds(b, gdim, stride=2), :] = parts[r][b]
    rows = []
    for r in range(2):
        cols = []
        for b in range(2):
            to_low = woven[r, b * gdim : (b + 1) * gdim, :]
            to_high = plain[r, pl.ds(b, gdim, stride=2), :]
            moved = jnp.where(old == 1, to_low, to_high)
            cols.append(jnp.where(old == new, parts[r][b], moved))
        rows.append(jnp.concatenate(cols, axis=1))
    return jnp.concatenate(rows, axis=0)


def run_gates(planes, mats, marks, plain, woven):
    gdim = planes[0].shape[0] // 2
    y = jnp.concatenate(
        [jnp.concatenate([p[:gdim], p[gdim:]], axis=1) for p in planes], axis=0
    )
    old = jnp.int32(0)
    for mat, new in zip(mats, marks):
        y = product(mat(), relayout(y, plain, woven, old, new))
        old = new
    y = relayout(y, plain, woven, old, jnp.int32(0))
    lanes = y.shape[1] // 2
    return [
        jnp.concatenate(
            [y[r * gdim : (r + 1) * gdim, :lanes], y[r * gdim : (r + 1) * gdim, lanes:]],
            axis=0,
        )
        for r in range(2)
    ]


def mix_pair(pair, p, b, low, high):
    r0, i0 = pair[p, 0, b, 0], pair[p, 1, b, 0]
    r1, i1 = pair[p, 0, b, 1], pair[p, 1, b, 1]
    re = r0 * low[0] - i0 * low[1] + (r1 * high[0] - i1 * high[1])
    im = r0 * low[1] + i0 * low[0] + (r1 * high[1] + i1 * high[0])
    return re, im


def compose(third, count, order, starts, u, plain, woven, w_hi, w_lo, after):
    rows, lanes = plain.shape[2], plain.shape[3]
    ks = [third * count + j for j in range(count)]
    built = [gate_matrix(u, order, k) for k in ks]
    for n in range(rows // lanes):
        at = lax.broadcasted_iota(jnp.int32, (rows, lanes), 0)
        col = lax.broadcasted_iota(jnp.int32, (rows, lanes), 1) + n * lanes
        one = jnp.where(at == col, 1.0, 0.0).astype(F32)
        planes = run_gates(
            [one, jnp.zeros_like(one)],
            [lambda m=m: m for m in built],
            [starts[k] for k in ks],
            plain.at[n],
            woven.at[n],
        )
        re, im = after(planes)
        for out, r, i in zip((w_hi, w_lo), split(re), split(im)):
            here = slice(n * lanes, (n + 1) * lanes)
            there = slice(rows + n * lanes, rows + (n + 1) * lanes)
            out[:rows, here] = r
            out[rows:, there] = r
            out[rows:, here] = i
            out[:rows, there] = -i


def apply(w_hi, w_lo, x):
    lanes = x.shape[1]
    x_hi, x_lo = split(x)
    both = dot(w_hi[...], jnp.concatenate([x_hi, x_lo], axis=1))
    return both[:, :lanes] + both[:, lanes:] + dot(w_lo[...], x_hi)


def kernel(
    group, pair_bit, order_hbm, starts_hbm, pair_hbm, x_hbm, u_hbm, x_out,
    order, starts, pair, x_in, u, first_hi, first_lo, plain, woven, w_hi, w_lo,
    sent, got, raw_got, mid_sent, mid_got, back, final,
    in_sem, send_sem, recv_sem, mid_send, mid_recv, raw_send, raw_recv,
):
    chunks, rows, lanes = x_in.shape[0], x_in.shape[1] // 2, x_in.shape[2]
    count = u.shape[0] // 3
    block = rows // group
    half, sub_group = chunks // 2, group // 2
    index = lax.axis_index("qa")
    me = lax.rem(index, group)
    base = index - me
    top, sub = me // sub_group, lax.rem(me, sub_group)

    small = [
        pltpu.make_async_copy(src, dst, in_sem.at[n])
        for n, (src, dst) in enumerate(
            [(order_hbm, order), (starts_hbm, starts), (pair_hbm, pair)]
        )
    ]
    load_u = pltpu.make_async_copy(u_hbm, u, in_sem.at[3])
    load_x = pltpu.make_async_copy(x_hbm, x_in, in_sem.at[4])
    barrier = pltpu.get_barrier_semaphore()
    for d in range(1, group):
        pl.semaphore_signal(
            barrier, inc=1, device_id={"qa": base + lax.rem(me + d, group)},
            device_id_type=pl.DeviceIdType.MESH,
        )
    for load in small + [load_u, load_x]:
        load.start()

    def copy_to(peer, src, dst, send, recv):
        return pltpu.make_async_remote_copy(
            src_ref=src, dst_ref=dst, send_sem=send, recv_sem=recv,
            device_id={"qa": base + peer}, device_id_type=pl.DeviceIdType.MESH,
        )

    partner = lax.rem(me + sub_group, group)
    raw = copy_to(
        partner, x_hbm.at[(1 - top) * half], raw_got, raw_send.at[0], raw_recv.at[0]
    )
    ret = copy_to(partner, back, final.at[top], raw_send.at[1], raw_recv.at[1])

    def block_at(j):
        return pl.ds(pl.multiple_of(j * block, block), block)

    def remote(phase, c, d):
        peer = lax.rem(me + d, group)
        return copy_to(
            peer,
            sent.at[phase, c, :, block_at(peer), :],
            got.at[phase, c, :, block_at(me), :],
            send_sem.at[phase, c, d],
            recv_sem.at[phase, c, d],
        )

    def exchange(phase, c):
        def one(d, _):
            remote(phase, c, d).start()
            return 0

        lax.fori_loop(1, group, one, 0)
        got[phase, c, :, block_at(me), :] = sent[phase, c, :, block_at(me), :]

    def arrived(phase, c):
        def one(d, _):
            remote(phase, c, d).wait_recv()
            return 0

        lax.fori_loop(1, group, one, 0)

    def middle(phase, d):
        peer = lax.rem(sub + d, sub_group)
        return copy_to(
            top * sub_group + peer,
            mid_sent.at[phase, :, block_at(peer), :],
            mid_got.at[phase, :, block_at(sub), :],
            mid_send.at[phase, d],
            mid_recv.at[phase, d],
        )

    def middle_exchange(phase):
        def one(d, _):
            middle(phase, d).start()
            return 0

        lax.fori_loop(1, sub_group, one, 0)
        mid_got[phase, :, block_at(sub), :] = mid_sent[phase, :, block_at(sub), :]

    def middle_arrived(phase):
        def one(d, _):
            middle(phase, d).wait_recv()
            return 0

        lax.fori_loop(1, sub_group, one, 0)

    def first_third(planes):
        return run_gates(
            planes,
            [lambda k=k: (first_hi[k], first_lo[k]) for k in range(count)],
            [starts[k] for k in range(count)],
            plain.at[0],
            woven.at[0],
        )

    def planes_of(ref):
        return [ref[pl.ds(r, rows, stride=2), :] for r in range(2)]

    pl.semaphore_wait(barrier, group - 1)
    raw.start()
    for load in small + [load_u]:
        load.wait()
    for k in range(count):
        first_hi[k], first_lo[k] = gate_matrix(u, order, k)
    load_x.wait()

    others = [c for c in range(chunks) if c % half]

    def first(i, _):
        b, low = i // (half - 1), 1 + lax.rem(i, half - 1)
        c = b * half + low
        done = first_third(
            mix_pair(pair, 0, b, planes_of(x_in.at[low]), planes_of(x_in.at[low + half]))
        )
        for r in range(2):
            sent[0, c, r] = done[r]
        exchange(0, c)
        return 0

    lax.fori_loop(0, len(others), first, 0)

    def first_raw(source, ref):
        done = first_third(planes_of(ref))
        for s in range(2):
            for r in range(2):
                part = done[r][s * rows // 2 : (s + 1) * rows // 2]
                mid_sent[0, s * 4 + r * 2 + source] = part

    first_raw(top, x_in.at[top * half])

    def with_pair(planes):
        pieces = ([], [])
        for start in range(0, rows, 2 * pair_bit):
            low = [p[start : start + pair_bit] for p in planes]
            high = [p[start + pair_bit : start + 2 * pair_bit] for p in planes]
            for b in range(2):
                for out, part in zip(pieces, mix_pair(pair, 1, b, low, high)):
                    out.append(part)
        return [jnp.concatenate(p, axis=0) for p in pieces]

    compose(1, count, order, starts, u, plain, woven, w_hi, w_lo, with_pair)

    def second(c):
        arrived(0, c)
        y = apply(w_hi, w_lo, got[0, c].reshape(2 * rows, lanes))
        sent[1, c] = y.reshape(2, rows, lanes)
        exchange(1, c)

    early = len(others) // 2
    for c in others[:early]:
        second(c)
    raw.wait_recv()
    first_raw(1 - top, raw_got)
    middle_exchange(0)
    for c in others[early:]:
        second(c)
    middle_arrived(0)
    for s in range(2):
        here = slice(4 * s, 4 * s + 4)
        y = apply(w_hi, w_lo, mid_got[0, here].reshape(2 * rows, lanes))
        mid_sent[1, here] = y.reshape(4, rows // 2, lanes)
    middle_exchange(1)

    compose(2, count, order, starts, u, plain, woven, w_hi, w_lo, lambda p: p)

    middle_arrived(1)

    def last_raw(source):
        parts = [mid_got[1, s * 4 + r * 2 + source] for r in range(2) for s in range(2)]
        y = apply(w_hi, w_lo, jnp.concatenate(parts, axis=0))
        return y.reshape(2, rows, lanes)

    back[...] = last_raw(1 - top)
    ret.start()
    final[top] = last_raw(top)

    for c in others:
        arrived(1, c)
        y = apply(w_hi, w_lo, got[1, c].reshape(2 * rows, lanes))
        for r in range(2):
            x_out[c, pl.ds(r, rows, stride=2), :] = y[r * rows : (r + 1) * rows]

    ret.wait_recv()
    for b in range(2):
        low, high = [[final[n, r] for r in range(2)] for n in range(2)]
        for r, plane in enumerate(mix_pair(pair, 0, b, low, high)):
            x_out[b * half, pl.ds(r, rows, stride=2), :] = plane

    raw.wait_send()
    ret.wait_send()
    for phase in range(2):
        lax.fori_loop(
            1, sub_group, lambda d, _: (middle(phase, d).wait_send(), 0)[1], 0
        )
        for c in others:
            lax.fori_loop(
                1, group, lambda d, _: (remote(phase, c, d).wait_send(), 0)[1], 0
            )


def shards(state, unitaries, gate_order, gate_starts, pair_gates):
    amp_local = state.shape[1]
    gdim = unitaries.shape[-1]
    ngates = unitaries.shape[0]
    rows, lanes = 2 * gdim, gdim
    chunks = amp_local // (rows * lanes)
    unit = amp_local // lax.axis_size("qa")
    group = rows * lanes // unit
    x = state.reshape(2, chunks * rows, lanes).transpose(1, 0, 2)
    x = x.reshape(chunks, 2 * rows, lanes)
    hbm = pl.BlockSpec(memory_space=pltpu.HBM)
    y = pl.pallas_call(
        functools.partial(kernel, group, unit // lanes),
        out_shape=pltpu.VMEM(x.shape, F32),
        in_specs=[hbm] * 5,
        out_specs=pl.BlockSpec(memory_space=pltpu.VMEM),
        scratch_shapes=[
            pltpu.SMEM(gate_order.shape, jnp.int32),
            pltpu.SMEM(gate_starts.shape, jnp.int32),
            pltpu.SMEM(pair_gates.shape, F32),
            pltpu.VMEM(x.shape, F32),
            pltpu.VMEM(unitaries.shape, F32),
            pltpu.VMEM((ngates // 3, 2 * gdim, 2 * gdim), BF16),
            pltpu.VMEM((ngates // 3, 2 * gdim, 2 * gdim), BF16),
            pltpu.VMEM((rows // lanes, 2, rows, lanes), F32),
            pltpu.VMEM((rows // lanes, 2, rows, lanes), F32),
            pltpu.VMEM((2 * rows, 2 * rows), BF16),
            pltpu.VMEM((2 * rows, 2 * rows), BF16),
            pltpu.VMEM((2, chunks, 2, rows, lanes), F32),
            pltpu.VMEM((2, chunks, 2, rows, lanes), F32),
            pltpu.VMEM((2 * rows, lanes), F32),
            pltpu.VMEM((2, 8, rows // 2, lanes), F32),
            pltpu.VMEM((2, 8, rows // 2, lanes), F32),
            pltpu.VMEM((2, rows, lanes), F32),
            pltpu.VMEM((2, 2, rows, lanes), F32),
            pltpu.SemaphoreType.DMA((5,)),
            pltpu.SemaphoreType.DMA((2, chunks, group)),
            pltpu.SemaphoreType.DMA((2, chunks, group)),
            pltpu.SemaphoreType.DMA((2, group // 2)),
            pltpu.SemaphoreType.DMA((2, group // 2)),
            pltpu.SemaphoreType.DMA((2,)),
            pltpu.SemaphoreType.DMA((2,)),
        ],
        compiler_params=pltpu.CompilerParams(
            collective_id=0, has_side_effects=True, vmem_limit_bytes=VMEM
        ),
        cost_estimate=pl.CostEstimate(
            flops=8 * 14 * chunks * rows * lanes * gdim,
            bytes_accessed=8 * amp_local * 2, transcendentals=0,
        ),
    )(*(
        pltpu.with_memory_space_constraint(a, pltpu.HBM)
        for a in (gate_order, gate_starts, pair_gates, x, unitaries)
    ))
    y = y.reshape(chunks * rows, 2, lanes).transpose(1, 0, 2)
    return y.reshape(2, amp_local)


def solution(mesh):
    placed = (P(None, ("cuts", "qa")), P(), P(), P(), P())
    return jax.shard_map(
        shards, mesh=mesh, in_specs=placed, out_specs=P(None, ("cuts", "qa")), check_vma=False
    )
```

```python
import functools

import jax
import jax.numpy as jnp
from jax import lax
from jax.experimental import pallas as pl
from jax.experimental.pallas import tpu as pltpu
from jax.sharding import PartitionSpec as P

VMEM = 40 * 2**20
BF16 = jnp.bfloat16
F32 = jnp.float32


def split(x):
    hi = x.astype(BF16)
    return hi, (x - hi.astype(F32)).astype(BF16)


def dot(a, b):
    return jnp.dot(a, b, preferred_element_type=F32)


def embed(re, im):
    return jnp.concatenate(
        [jnp.concatenate([re, -im], axis=1), jnp.concatenate([im, re], axis=1)], axis=0
    )


def gate_matrix(u, order, k):
    re_hi, re_lo = split(u[order[k], 0])
    im_hi, im_lo = split(u[order[k], 1])
    return embed(re_hi, im_hi), embed(re_lo, im_lo)


def product(mat, x):
    hi, lo = mat
    x_hi, x_lo = split(x)
    return dot(hi, x_hi) + dot(hi, x_lo) + dot(lo, x_hi)


def relayout(y, plain, woven, old, new):
    gdim, lanes = y.shape[0] // 2, y.shape[1] // 2
    parts = [
        [y[r * gdim : (r + 1) * gdim, b * lanes : (b + 1) * lanes] for b in range(2)]
        for r in range(2)
    ]
    for r in range(2):
        for b in range(2):
            plain[r, b * gdim : (b + 1) * gdim, :] = parts[r][b]
            woven[r, pl.ds(b, gdim, stride=2), :] = parts[r][b]
    rows = []
    for r in range(2):
        cols = []
        for b in range(2):
            to_low = woven[r, b * gdim : (b + 1) * gdim, :]
            to_high = plain[r, pl.ds(b, gdim, stride=2), :]
            moved = jnp.where(old == 1, to_low, to_high)
            cols.append(jnp.where(old == new, parts[r][b], moved))
        rows.append(jnp.concatenate(cols, axis=1))
    return jnp.concatenate(rows, axis=0)


def run_gates(planes, mats, marks, plain, woven):
    gdim = planes[0].shape[0] // 2
    y = jnp.concatenate(
        [jnp.concatenate([p[:gdim], p[gdim:]], axis=1) for p in planes], axis=0
    )
    old = jnp.int32(0)
    for mat, new in zip(mats, marks):
        y = product(mat(), relayout(y, plain, woven, old, new))
        old = new
    y = relayout(y, plain, woven, old, jnp.int32(0))
    lanes = y.shape[1] // 2
    return [
        jnp.concatenate(
            [y[r * gdim : (r + 1) * gdim, :lanes], y[r * gdim : (r + 1) * gdim, lanes:]],
            axis=0,
        )
        for r in range(2)
    ]


def mix_pair(pair, p, b, low, high):
    r0, i0 = pair[p, 0, b, 0], pair[p, 1, b, 0]
    r1, i1 = pair[p, 0, b, 1], pair[p, 1, b, 1]
    re = r0 * low[0] - i0 * low[1] + (r1 * high[0] - i1 * high[1])
    im = r0 * low[1] + i0 * low[0] + (r1 * high[1] + i1 * high[0])
    return re, im


def compose(third, count, order, starts, u, plain, woven, w_hi, w_lo, after):
    rows, lanes = plain.shape[2], plain.shape[3]
    ks = [third * count + j for j in range(count)]
    built = [gate_matrix(u, order, k) for k in ks]
    for n in range(rows // lanes):
        at = lax.broadcasted_iota(jnp.int32, (rows, lanes), 0)
        col = lax.broadcasted_iota(jnp.int32, (rows, lanes), 1) + n * lanes
        one = jnp.where(at == col, 1.0, 0.0).astype(F32)
        planes = run_gates(
            [one, jnp.zeros_like(one)],
            [lambda m=m: m for m in built],
            [starts[k] for k in ks],
            plain.at[n],
            woven.at[n],
        )
        re, im = after(planes)
        for out, r, i in zip((w_hi, w_lo), split(re), split(im)):
            here = slice(n * lanes, (n + 1) * lanes)
            there = slice(rows + n * lanes, rows + (n + 1) * lanes)
            out[:rows, here] = r
            out[rows:, there] = r
            out[rows:, here] = i
            out[:rows, there] = -i


def apply(w_hi, w_lo, x):
    lanes = x.shape[1]
    x_hi, x_lo = split(x)
    both = dot(w_hi[...], jnp.concatenate([x_hi, x_lo], axis=1))
    return both[:, :lanes] + both[:, lanes:] + dot(w_lo[...], x_hi)


def kernel(
    group, pair_bit, order_hbm, starts_hbm, pair_hbm, x_hbm, u_hbm, x_out,
    order, starts, pair, x_in, u, first_hi, first_lo, plain, woven, w_hi, w_lo,
    sent, got, raw_got, mid_sent, mid_got, back, final,
    in_sem, send_sem, recv_sem, mid_send, mid_recv, raw_send, raw_recv,
):
    chunks, rows, lanes = x_in.shape[0], x_in.shape[1] // 2, x_in.shape[2]
    count = u.shape[0] // 3
    block = rows // group
    half, sub_group = chunks // 2, group // 2
    index = lax.axis_index("qa")
    me = lax.rem(index, group)
    base = index - me
    top, sub = me // sub_group, lax.rem(me, sub_group)

    small = [
        pltpu.make_async_copy(src, dst, in_sem.at[n])
        for n, (src, dst) in enumerate(
            [(order_hbm, order), (starts_hbm, starts), (pair_hbm, pair)]
        )
    ]
    load_u = pltpu.make_async_copy(u_hbm, u, in_sem.at[3])
    load_x = pltpu.make_async_copy(x_hbm, x_in, in_sem.at[4])
    barrier = pltpu.get_barrier_semaphore()
    for d in range(1, group):
        pl.semaphore_signal(
            barrier, inc=1, device_id={"qa": base + lax.rem(me + d, group)},
            device_id_type=pl.DeviceIdType.MESH,
        )
    for load in small + [load_u, load_x]:
        load.start()

    def copy_to(peer, src, dst, send, recv):
        return pltpu.make_async_remote_copy(
            src_ref=src, dst_ref=dst, send_sem=send, recv_sem=recv,
            device_id={"qa": base + peer}, device_id_type=pl.DeviceIdType.MESH,
        )

    partner = lax.rem(me + sub_group, group)
    raw = copy_to(
        partner, x_hbm.at[(1 - top) * half], raw_got, raw_send.at[0], raw_recv.at[0]
    )
    ret = copy_to(partner, back, final.at[top], raw_send.at[1], raw_recv.at[1])

    def block_at(j):
        return pl.ds(pl.multiple_of(j * block, block), block)

    def remote(phase, c, d):
        peer = lax.rem(me + d, group)
        return copy_to(
            peer,
            sent.at[phase, c, :, block_at(peer), :],
            got.at[phase, c, :, block_at(me), :],
            send_sem.at[phase, c, d],
            recv_sem.at[phase, c, d],
        )

    def exchange(phase, c):
        def one(d, _):
            remote(phase, c, d).start()
            return 0

        lax.fori_loop(1, group, one, 0)
        got[phase, c, :, block_at(me), :] = sent[phase, c, :, block_at(me), :]

    def arrived(phase, c):
        def one(d, _):
            remote(phase, c, d).wait_recv()
            return 0

        lax.fori_loop(1, group, one, 0)

    def middle(phase, s, d):
        peer = lax.rem(sub + d, sub_group)
        here = pl.ds(4 * s, 4)
        return copy_to(
            top * sub_group + peer,
            mid_sent.at[phase, here, block_at(peer), :],
            mid_got.at[phase, here, block_at(sub), :],
            mid_send.at[phase, s, d],
            mid_recv.at[phase, s, d],
        )

    def middle_exchange(phase, s):
        def one(d, _):
            middle(phase, s, d).start()
            return 0

        lax.fori_loop(1, sub_group, one, 0)
        here = slice(4 * s, 4 * s + 4)
        mid_got[phase, here, block_at(sub), :] = mid_sent[phase, here, block_at(sub), :]

    def middle_arrived(phase, s):
        def one(d, _):
            middle(phase, s, d).wait_recv()
            return 0

        lax.fori_loop(1, sub_group, one, 0)

    def first_third(planes):
        return run_gates(
            planes,
            [lambda k=k: (first_hi[k], first_lo[k]) for k in range(count)],
            [starts[k] for k in range(count)],
            plain.at[0],
            woven.at[0],
        )

    def planes_of(ref):
        return [ref[pl.ds(r, rows, stride=2), :] for r in range(2)]

    pl.semaphore_wait(barrier, group - 1)
    raw.start()
    for load in small + [load_u]:
        load.wait()
    for k in range(count):
        first_hi[k], first_lo[k] = gate_matrix(u, order, k)
    load_x.wait()

    others = [c for c in range(chunks) if c % half]

    def first(i, _):
        b, low = i // (half - 1), 1 + lax.rem(i, half - 1)
        c = b * half + low
        done = first_third(
            mix_pair(pair, 0, b, planes_of(x_in.at[low]), planes_of(x_in.at[low + half]))
        )
        for r in range(2):
            sent[0, c, r] = done[r]
        exchange(0, c)
        return 0

    lax.fori_loop(0, len(others), first, 0)

    def first_raw(source, ref):
        done = first_third(planes_of(ref))
        for s in range(2):
            for r in range(2):
                part = done[r][s * rows // 2 : (s + 1) * rows // 2]
                mid_sent[0, s * 4 + r * 2 + source] = part

    first_raw(top, x_in.at[top * half])

    def with_pair(planes):
        pieces = ([], [])
        for start in range(0, rows, 2 * pair_bit):
            low = [p[start : start + pair_bit] for p in planes]
            high = [p[start + pair_bit : start + 2 * pair_bit] for p in planes]
            for b in range(2):
                for out, part in zip(pieces, mix_pair(pair, 1, b, low, high)):
                    out.append(part)
        return [jnp.concatenate(p, axis=0) for p in pieces]

    compose(1, count, order, starts, u, plain, woven, w_hi.at[0], w_lo.at[0], with_pair)
    compose(2, count, order, starts, u, plain, woven, w_hi.at[1], w_lo.at[1], lambda p: p)

    def second(c):
        arrived(0, c)
        y = apply(w_hi.at[0], w_lo.at[0], got[0, c].reshape(2 * rows, lanes))
        sent[1, c] = y.reshape(2, rows, lanes)
        exchange(1, c)

    early = len(others) // 2
    for c in others[:early]:
        second(c)
    raw.wait_recv()
    first_raw(1 - top, raw_got)
    for s in range(2):
        middle_exchange(0, s)
    for c in others[early:]:
        second(c)
    for s in range(2):
        middle_arrived(0, s)
        here = slice(4 * s, 4 * s + 4)
        y = apply(w_hi.at[0], w_lo.at[0], mid_got[0, here].reshape(2 * rows, lanes))
        mid_sent[1, here] = y.reshape(4, rows // 2, lanes)
        middle_exchange(1, s)

    for s in range(2):
        middle_arrived(1, s)

    def last_raw(source):
        parts = [mid_got[1, s * 4 + r * 2 + source] for r in range(2) for s in range(2)]
        y = apply(w_hi.at[1], w_lo.at[1], jnp.concatenate(parts, axis=0))
        return y.reshape(2, rows, lanes)

    back[...] = last_raw(1 - top)
    ret.start()
    final[top] = last_raw(top)

    for c in others:
        arrived(1, c)
        y = apply(w_hi.at[1], w_lo.at[1], got[1, c].reshape(2 * rows, lanes))
        for r in range(2):
            x_out[c, pl.ds(r, rows, stride=2), :] = y[r * rows : (r + 1) * rows]

    ret.wait_recv()
    for b in range(2):
        low, high = [[final[n, r] for r in range(2)] for n in range(2)]
        for r, plane in enumerate(mix_pair(pair, 0, b, low, high)):
            x_out[b * half, pl.ds(r, rows, stride=2), :] = plane

    raw.wait_send()
    ret.wait_send()
    for phase in range(2):
        for s in range(2):
            lax.fori_loop(
                1, sub_group, lambda d, _: (middle(phase, s, d).wait_send(), 0)[1], 0
            )
        for c in others:
            lax.fori_loop(
                1, group, lambda d, _: (remote(phase, c, d).wait_send(), 0)[1], 0
            )


def shards(state, unitaries, gate_order, gate_starts, pair_gates):
    amp_local = state.shape[1]
    gdim = unitaries.shape[-1]
    ngates = unitaries.shape[0]
    rows, lanes = 2 * gdim, gdim
    chunks = amp_local // (rows * lanes)
    unit = amp_local // lax.axis_size("qa")
    group = rows * lanes // unit
    x = state.reshape(2, chunks * rows, lanes).transpose(1, 0, 2)
    x = x.reshape(chunks, 2 * rows, lanes)
    hbm = pl.BlockSpec(memory_space=pltpu.HBM)
    y = pl.pallas_call(
        functools.partial(kernel, group, unit // lanes),
        out_shape=pltpu.VMEM(x.shape, F32),
        in_specs=[hbm] * 5,
        out_specs=pl.BlockSpec(memory_space=pltpu.VMEM),
        scratch_shapes=[
            pltpu.SMEM(gate_order.shape, jnp.int32),
            pltpu.SMEM(gate_starts.shape, jnp.int32),
            pltpu.SMEM(pair_gates.shape, F32),
            pltpu.VMEM(x.shape, F32),
            pltpu.VMEM(unitaries.shape, F32),
            pltpu.VMEM((ngates // 3, 2 * gdim, 2 * gdim), BF16),
            pltpu.VMEM((ngates // 3, 2 * gdim, 2 * gdim), BF16),
            pltpu.VMEM((rows // lanes, 2, rows, lanes), F32),
            pltpu.VMEM((rows // lanes, 2, rows, lanes), F32),
            pltpu.VMEM((2, 2 * rows, 2 * rows), BF16),
            pltpu.VMEM((2, 2 * rows, 2 * rows), BF16),
            pltpu.VMEM((2, chunks, 2, rows, lanes), F32),
            pltpu.VMEM((2, chunks, 2, rows, lanes), F32),
            pltpu.VMEM((2 * rows, lanes), F32),
            pltpu.VMEM((2, 8, rows // 2, lanes), F32),
            pltpu.VMEM((2, 8, rows // 2, lanes), F32),
            pltpu.VMEM((2, rows, lanes), F32),
            pltpu.VMEM((2, 2, rows, lanes), F32),
            pltpu.SemaphoreType.DMA((5,)),
            pltpu.SemaphoreType.DMA((2, chunks, group)),
            pltpu.SemaphoreType.DMA((2, chunks, group)),
            pltpu.SemaphoreType.DMA((2, 2, group // 2)),
            pltpu.SemaphoreType.DMA((2, 2, group // 2)),
            pltpu.SemaphoreType.DMA((2,)),
            pltpu.SemaphoreType.DMA((2,)),
        ],
        compiler_params=pltpu.CompilerParams(
            collective_id=0, has_side_effects=True, vmem_limit_bytes=VMEM
        ),
        cost_estimate=pl.CostEstimate(
            flops=8 * 14 * chunks * rows * lanes * gdim,
            bytes_accessed=8 * amp_local * 2, transcendentals=0,
        ),
    )(*(
        pltpu.with_memory_space_constraint(a, pltpu.HBM)
        for a in (gate_order, gate_starts, pair_gates, x, unitaries)
    ))
    y = y.reshape(chunks * rows, 2, lanes).transpose(1, 0, 2)
    return y.reshape(2, amp_local)


def solution(mesh):
    placed = (P(None, ("cuts", "qa")), P(), P(), P(), P())
    return jax.shard_map(
        shards, mesh=mesh, in_specs=placed, out_specs=P(None, ("cuts", "qa")), check_vma=False
    )
```

```python
import functools

import jax
import jax.numpy as jnp
from jax import lax
from jax.experimental import pallas as pl
from jax.experimental.pallas import tpu as pltpu
from jax.sharding import PartitionSpec as P

VMEM = 40 * 2**20
BF16 = jnp.bfloat16
F32 = jnp.float32


def split(x):
    hi = x.astype(BF16)
    return hi, (x - hi.astype(F32)).astype(BF16)


def dot(a, b):
    return jnp.dot(a, b, preferred_element_type=F32)


def embed(re, im):
    return jnp.concatenate(
        [jnp.concatenate([re, -im], axis=1), jnp.concatenate([im, re], axis=1)], axis=0
    )


def gate_matrix(u, order, k):
    re_hi, re_lo = split(u[order[k], 0])
    im_hi, im_lo = split(u[order[k], 1])
    return jnp.concatenate([embed(re_hi, im_hi), embed(re_lo, im_lo)], axis=0)


def product(mat, x):
    size = mat.shape[1]
    x_hi, x_lo = split(x)
    both = dot(mat, x_hi)
    return both[:size] + both[size:] + dot(mat[:size], x_lo)


def relayout(y, plain, woven, old, new):
    gdim, lanes = y.shape[0] // 2, y.shape[1] // 2
    parts = [
        [y[r * gdim : (r + 1) * gdim, b * lanes : (b + 1) * lanes] for b in range(2)]
        for r in range(2)
    ]
    for r in range(2):
        for b in range(2):
            plain[r, b * gdim : (b + 1) * gdim, :] = parts[r][b]
            woven[r, pl.ds(b, gdim, stride=2), :] = parts[r][b]
    rows = []
    for r in range(2):
        cols = []
        for b in range(2):
            to_low = woven[r, b * gdim : (b + 1) * gdim, :]
            to_high = plain[r, pl.ds(b, gdim, stride=2), :]
            moved = jnp.where(old == 1, to_low, to_high)
            cols.append(jnp.where(old == new, parts[r][b], moved))
        rows.append(jnp.concatenate(cols, axis=1))
    return jnp.concatenate(rows, axis=0)


def run_gates(planes, mats, marks, plain, woven):
    gdim = planes[0].shape[0] // 2
    y = jnp.concatenate(
        [jnp.concatenate([p[:gdim], p[gdim:]], axis=1) for p in planes], axis=0
    )
    old = jnp.int32(0)
    for mat, new in zip(mats, marks):
        y = product(mat(), relayout(y, plain, woven, old, new))
        old = new
    y = relayout(y, plain, woven, old, jnp.int32(0))
    lanes = y.shape[1] // 2
    return [
        jnp.concatenate(
            [y[r * gdim : (r + 1) * gdim, :lanes], y[r * gdim : (r + 1) * gdim, lanes:]],
            axis=0,
        )
        for r in range(2)
    ]


def mix_pair(pair, p, b, low, high):
    r0, i0 = pair[p, 0, b, 0], pair[p, 1, b, 0]
    r1, i1 = pair[p, 0, b, 1], pair[p, 1, b, 1]
    re = r0 * low[0] - i0 * low[1] + (r1 * high[0] - i1 * high[1])
    im = r0 * low[1] + i0 * low[0] + (r1 * high[1] + i1 * high[0])
    return re, im


def compose(third, count, n, order, starts, u, plain, woven, after):
    rows, lanes = plain.shape[1], plain.shape[2]
    ks = [third * count + j for j in range(count)]
    at = lax.broadcasted_iota(jnp.int32, (rows, lanes), 0)
    col = lax.broadcasted_iota(jnp.int32, (rows, lanes), 1) + n * lanes
    one = jnp.where(at == col, 1.0, 0.0).astype(F32)
    planes = run_gates(
        [one, jnp.zeros_like(one)],
        [lambda k=k: gate_matrix(u, order, k) for k in ks],
        [starts[k] for k in ks],
        plain,
        woven,
    )
    return after(planes)


def place(columns, w_hi, w_lo):
    blocks, _, rows, lanes = columns.shape
    for n in range(blocks):
        for out, r, i in zip((w_hi, w_lo), split(columns[n, 0]), split(columns[n, 1])):
            here = slice(n * lanes, (n + 1) * lanes)
            there = slice(rows + n * lanes, rows + (n + 1) * lanes)
            out[:rows, here] = r
            out[rows:, there] = r
            out[rows:, here] = i
            out[:rows, there] = -i


def apply(w_hi, w_lo, x):
    lanes = x.shape[1]
    x_hi, x_lo = split(x)
    both = dot(w_hi[...], jnp.concatenate([x_hi, x_lo], axis=1))
    return both[:, :lanes] + both[:, lanes:] + dot(w_lo[...], x_hi)


def kernel(
    group, pair_bit, order_hbm, starts_hbm, pair_hbm, x_hbm, u_hbm, x_out,
    order, starts, pair, x_in, u, first_mat, columns, plain, woven, w_hi, w_lo,
    sent, got, raw_got, mid_sent, mid_got, back, final,
    in_sem, send_sem, recv_sem, mid_send, mid_recv, raw_send, raw_recv,
    share_send, share_recv,
):
    chunks, rows, lanes = x_in.shape[0], x_in.shape[1] // 2, x_in.shape[2]
    count = u.shape[0] // 3
    block = rows // group
    half, sub_group = chunks // 2, group // 2
    index = lax.axis_index("qa")
    me = lax.rem(index, group)
    base = index - me
    top, sub = me // sub_group, lax.rem(me, sub_group)

    small = [
        pltpu.make_async_copy(src, dst, in_sem.at[n])
        for n, (src, dst) in enumerate(
            [(order_hbm, order), (starts_hbm, starts), (pair_hbm, pair)]
        )
    ]
    load_u = pltpu.make_async_copy(u_hbm, u, in_sem.at[3])
    load_x = pltpu.make_async_copy(x_hbm, x_in, in_sem.at[4])
    barrier = pltpu.get_barrier_semaphore()
    for d in range(1, group):
        pl.semaphore_signal(
            barrier, inc=1, device_id={"qa": base + lax.rem(me + d, group)},
            device_id_type=pl.DeviceIdType.MESH,
        )
    for load in small + [load_u, load_x]:
        load.start()

    def copy_to(peer, src, dst, send, recv):
        return pltpu.make_async_remote_copy(
            src_ref=src, dst_ref=dst, send_sem=send, recv_sem=recv,
            device_id={"qa": base + peer}, device_id_type=pl.DeviceIdType.MESH,
        )

    partner = lax.rem(me + sub_group, group)
    raw = copy_to(
        partner, x_hbm.at[(1 - top) * half], raw_got, raw_send.at[0], raw_recv.at[0]
    )
    ret = copy_to(partner, back, final.at[top], raw_send.at[1], raw_recv.at[1])

    def block_at(j):
        return pl.ds(pl.multiple_of(j * block, block), block)

    def remote(phase, c, d):
        peer = lax.rem(me + d, group)
        return copy_to(
            peer,
            sent.at[phase, c, :, block_at(peer), :],
            got.at[phase, c, :, block_at(me), :],
            send_sem.at[phase, c, d],
            recv_sem.at[phase, c, d],
        )

    def exchange(phase, c):
        def one(d, _):
            remote(phase, c, d).start()
            return 0

        lax.fori_loop(1, group, one, 0)
        got[phase, c, :, block_at(me), :] = sent[phase, c, :, block_at(me), :]

    def arrived(phase, c):
        def one(d, _):
            remote(phase, c, d).wait_recv()
            return 0

        lax.fori_loop(1, group, one, 0)

    def middle(phase, s, d):
        peer = lax.rem(sub + d, sub_group)
        here = pl.ds(4 * s, 4)
        return copy_to(
            top * sub_group + peer,
            mid_sent.at[phase, here, block_at(peer), :],
            mid_got.at[phase, here, block_at(sub), :],
            mid_send.at[phase, s, d],
            mid_recv.at[phase, s, d],
        )

    def middle_exchange(phase, s):
        def one(d, _):
            middle(phase, s, d).start()
            return 0

        lax.fori_loop(1, sub_group, one, 0)
        here = slice(4 * s, 4 * s + 4)
        mid_got[phase, here, block_at(sub), :] = mid_sent[phase, here, block_at(sub), :]

    def middle_arrived(phase, s):
        def one(d, _):
            middle(phase, s, d).wait_recv()
            return 0

        lax.fori_loop(1, sub_group, one, 0)

    def first_third(planes):
        return run_gates(
            planes,
            [lambda k=k: first_mat[k] for k in range(count)],
            [starts[k] for k in range(count)],
            plain,
            woven,
        )

    def planes_of(ref):
        return [ref[pl.ds(r, rows, stride=2), :] for r in range(2)]

    pl.semaphore_wait(barrier, group - 1)
    raw.start()
    for load in small + [load_u]:
        load.wait()
    for k in range(count):
        first_mat[k] = gate_matrix(u, order, k)
    load_x.wait()

    others = [c for c in range(chunks) if c % half]

    def first(i, _):
        b, low = i // (half - 1), 1 + lax.rem(i, half - 1)
        c = b * half + low
        done = first_third(
            mix_pair(pair, 0, b, planes_of(x_in.at[low]), planes_of(x_in.at[low + half]))
        )
        for r in range(2):
            sent[0, c, r] = done[r]
        exchange(0, c)
        return 0

    lax.fori_loop(0, len(others), first, 0)

    def first_raw(source, ref):
        done = first_third(planes_of(ref))
        for s in range(2):
            for r in range(2):
                part = done[r][s * rows // 2 : (s + 1) * rows // 2]
                mid_sent[0, s * 4 + r * 2 + source] = part

    first_raw(top, x_in.at[top * half])

    def with_pair(planes):
        pieces = ([], [])
        for start in range(0, rows, 2 * pair_bit):
            low = [p[start : start + pair_bit] for p in planes]
            high = [p[start + pair_bit : start + 2 * pair_bit] for p in planes]
            for b in range(2):
                for out, part in zip(pieces, mix_pair(pair, 1, b, low, high)):
                    out.append(part)
        return [jnp.concatenate(p, axis=0) for p in pieces]

    mine = lax.rem(me, 2)
    shares = [
        copy_to(
            me + 1 - 2 * mine, columns.at[t, mine], columns.at[t, mine],
            share_send.at[t], share_recv.at[t],
        )
        for t in range(2)
    ]
    for t, after in enumerate((with_pair, lambda p: p)):
        planes = compose(1 + t, count, mine, order, starts, u, plain, woven, after)
        for r in range(2):
            columns[t, mine, r] = planes[r]
        shares[t].start()

    def placed(t):
        shares[t].wait_recv()
        place(columns.at[t], w_hi.at[t], w_lo.at[t])

    placed(0)

    def second(c):
        arrived(0, c)
        y = apply(w_hi.at[0], w_lo.at[0], got[0, c].reshape(2 * rows, lanes))
        sent[1, c] = y.reshape(2, rows, lanes)
        exchange(1, c)

    early = len(others) // 2
    for c in others[:early]:
        second(c)
    placed(1)
    raw.wait_recv()
    first_raw(1 - top, raw_got)
    for s in range(2):
        middle_exchange(0, s)
    for c in others[early:]:
        second(c)
    for s in range(2):
        middle_arrived(0, s)
        here = slice(4 * s, 4 * s + 4)
        y = apply(w_hi.at[0], w_lo.at[0], mid_got[0, here].reshape(2 * rows, lanes))
        mid_sent[1, here] = y.reshape(4, rows // 2, lanes)
        middle_exchange(1, s)

    for s in range(2):
        middle_arrived(1, s)

    def last_raw(source):
        parts = [mid_got[1, s * 4 + r * 2 + source] for r in range(2) for s in range(2)]
        y = apply(w_hi.at[1], w_lo.at[1], jnp.concatenate(parts, axis=0))
        return y.reshape(2, rows, lanes)

    back[...] = last_raw(1 - top)
    ret.start()
    final[top] = last_raw(top)

    for c in others:
        arrived(1, c)
        y = apply(w_hi.at[1], w_lo.at[1], got[1, c].reshape(2 * rows, lanes))
        for r in range(2):
            x_out[c, pl.ds(r, rows, stride=2), :] = y[r * rows : (r + 1) * rows]

    ret.wait_recv()
    for b in range(2):
        low, high = [[final[n, r] for r in range(2)] for n in range(2)]
        for r, plane in enumerate(mix_pair(pair, 0, b, low, high)):
            x_out[b * half, pl.ds(r, rows, stride=2), :] = plane

    for share in shares:
        share.wait_send()
    raw.wait_send()
    ret.wait_send()
    for phase in range(2):
        for s in range(2):
            lax.fori_loop(
                1, sub_group, lambda d, _: (middle(phase, s, d).wait_send(), 0)[1], 0
            )
        for c in others:
            lax.fori_loop(
                1, group, lambda d, _: (remote(phase, c, d).wait_send(), 0)[1], 0
            )


def shards(state, unitaries, gate_order, gate_starts, pair_gates):
    amp_local = state.shape[1]
    gdim = unitaries.shape[-1]
    ngates = unitaries.shape[0]
    rows, lanes = 2 * gdim, gdim
    chunks = amp_local // (rows * lanes)
    unit = amp_local // lax.axis_size("qa")
    group = rows * lanes // unit
    x = state.reshape(2, chunks * rows, lanes).transpose(1, 0, 2)
    x = x.reshape(chunks, 2 * rows, lanes)
    hbm = pl.BlockSpec(memory_space=pltpu.HBM)
    y = pl.pallas_call(
        functools.partial(kernel, group, unit // lanes),
        out_shape=pltpu.VMEM(x.shape, F32),
        in_specs=[hbm] * 5,
        out_specs=pl.BlockSpec(memory_space=pltpu.VMEM),
        scratch_shapes=[
            pltpu.SMEM(gate_order.shape, jnp.int32),
            pltpu.SMEM(gate_starts.shape, jnp.int32),
            pltpu.SMEM(pair_gates.shape, F32),
            pltpu.VMEM(x.shape, F32),
            pltpu.VMEM(unitaries.shape, F32),
            pltpu.VMEM((ngates // 3, 4 * gdim, 2 * gdim), BF16),
            pltpu.VMEM((2, 2, 2, rows, lanes), F32),
            pltpu.VMEM((2, rows, lanes), F32),
            pltpu.VMEM((2, rows, lanes), F32),
            pltpu.VMEM((2, 2 * rows, 2 * rows), BF16),
            pltpu.VMEM((2, 2 * rows, 2 * rows), BF16),
            pltpu.VMEM((2, chunks, 2, rows, lanes), F32),
            pltpu.VMEM((2, chunks, 2, rows, lanes), F32),
            pltpu.VMEM((2 * rows, lanes), F32),
            pltpu.VMEM((2, 8, rows // 2, lanes), F32),
            pltpu.VMEM((2, 8, rows // 2, lanes), F32),
            pltpu.VMEM((2, rows, lanes), F32),
            pltpu.VMEM((2, 2, rows, lanes), F32),
            pltpu.SemaphoreType.DMA((5,)),
            pltpu.SemaphoreType.DMA((2, chunks, group)),
            pltpu.SemaphoreType.DMA((2, chunks, group)),
            pltpu.SemaphoreType.DMA((2, 2, group // 2)),
            pltpu.SemaphoreType.DMA((2, 2, group // 2)),
            pltpu.SemaphoreType.DMA((2,)),
            pltpu.SemaphoreType.DMA((2,)),
            pltpu.SemaphoreType.DMA((2,)),
            pltpu.SemaphoreType.DMA((2,)),
        ],
        compiler_params=pltpu.CompilerParams(
            collective_id=0, has_side_effects=True, vmem_limit_bytes=VMEM
        ),
        cost_estimate=pl.CostEstimate(
            flops=8 * 14 * chunks * rows * lanes * gdim,
            bytes_accessed=8 * amp_local * 2, transcendentals=0,
        ),
    )(*(
        pltpu.with_memory_space_constraint(a, pltpu.HBM)
        for a in (gate_order, gate_starts, pair_gates, x, unitaries)
    ))
    y = y.reshape(chunks * rows, 2, lanes).transpose(1, 0, 2)
    return y.reshape(2, amp_local)


def solution(mesh):
    placed = (P(None, ("cuts", "qa")), P(), P(), P(), P())
    return jax.shard_map(
        shards, mesh=mesh, in_specs=placed, out_specs=P(None, ("cuts", "qa")), check_vma=False
    )
```
